128 devices in a mesh: dp: 16 (over y, z_hi, core), expert: 8 (over z_lo, x).
Axes of the slice: x: 4, y: 4, z: 4 (z_hi: 2, z_lo: 2; z = z_hi * 2 + z_lo), core: 2. Of those that a mesh axis runs over, the one named last changes fastest.
Arguments:
- policy_hidden: bfloat16 [2048, 4096], P('dp', 'expert'), may hold values from -6 to 6
- reference_hidden: bfloat16 [2048, 4096], P('dp', 'expert'), may hold values from -6 to 6
- policy_norm_gain: float32 [4096], P('expert'), may hold values from 0.25 to 1.75
- reference_norm_gain: float32 [4096], P('expert'), may hold values from 0.25 to 1.75
- policy_router: float32 [4096, 8], P('expert'), may hold values from -5.1875 to 5.1875
- reference_router: float32 [4096, 8], P('expert'), may hold values from -5.1875 to 5.1875
- policy_gate: bfloat16 [8, 4096, 8192], P('expert', 'dp'), may hold values from -0.09375 to 0.09375
- policy_up: bfloat16 [8, 4096, 8192], P('expert', 'dp'), may hold values from -0.09375 to 0.09375
- policy_down: bfloat16 [8, 8192, 4096], P('expert', 'dp'), may hold values from -0.0625 to 0.0625
- reference_gate: bfloat16 [8, 4096, 8192], P('expert', 'dp'), may hold values from -0.09375 to 0.09375
- reference_up: bfloat16 [8, 4096, 8192], P('expert', 'dp'), may hold values from -0.09375 to 0.09375
- reference_down: bfloat16 [8, 8192, 4096], P('expert', 'dp'), may hold values from -0.0625 to 0.0625
- expert_ids: int32 [2048, 2], P('dp'), may hold values from 0 to 7, all different within a row; in each aligned block of 128 rows (0 to 127, 128 to 255, ...) at most 48 rows name the same one
- lengths: int32 [64], P('dp'), may hold values from 1 to 32, as said below
Outputs:
- policy_mixture: bfloat16 [2048, 4096], P('dp', 'expert')
- reference_mixture: bfloat16 [2048, 4096], P('dp', 'expert')
- token_kl: float32 [2048], P('dp')
- loss: float32 [], replicated
The draws below stay inside these ranges and needn't reach their ends.
Inputs may be any that keep to these rules, and one draw needn't show every extreme that they name: `expert_ids`: each row names 2 different experts; among the rows of one index of dp (aligned blocks of 128 rows) no expert is named more than 48 times, and in some block one expert is named exactly 48 times. The first lengths[r] of rollout r's 32 positions are live.
All inputs are finite; a program needn't handle non-finite values.
Results may differ from the reference program's by a relative error of at most 0.02.
Values may be sent and summed in bfloat16 or wider, within the bound.
No kernel may reach another device: no remote copies, remote signals or barrier semaphores. Data moves between devices by JAX's collectives and lax.ppermute only.
A program may use at most 256 MiB of HBM per device.

```python
import math
import jax
import jax.numpy as jnp
import numpy as np
from jax import lax

D = 4096
FF = 8192
TOP = 2
SEG = 32
TOK_DEV = 128
EXPERTS = 8
CAP = 48
TOKENS = 2048
N_DP = 16


def router_draw(key, stream_index):
    individual = jnp.clip(jax.random.normal(jax.random.fold_in(key, stream_index), (D, EXPERTS), jnp.float32), -4.0, 4.0) / math.sqrt(D)
    return individual


def draw_policy_router(key, part):
    return router_draw(key, 11)


def draw_reference_router(key, part):
    return router_draw(key, 12)


def draw_lengths(key, part):
    rollout_count = TOKENS // SEG
    per_block = TOK_DEV // SEG
    rollout_index = jnp.arange(rollout_count, dtype=jnp.int32)
    block_index = rollout_index // per_block
    block_total = rollout_count // per_block
    floor_limit = max(SEG // 3, 1)
    upper_limit = floor_limit + (SEG - floor_limit) * block_index // max(block_total - 1, 1)
    drawn = jax.random.randint(jax.random.fold_in(key, 5), (rollout_count,), 1, upper_limit + 1, dtype=jnp.int32)
    fullest = rollout_count - per_block
    drawn = jnp.where(rollout_index == fullest, jnp.int32(SEG), drawn)
    drawn = jnp.where(rollout_index == 0, jnp.int32(1), drawn)
    return drawn.astype(jnp.int32)


def levels(own_key, extent, pieces, low, high):
    level, own = 1.0, jax.random.fold_in(own_key, 6)
    for dim, parts in pieces:
        steps = jnp.exp(jax.random.uniform(jax.random.fold_in(own, dim), (parts,), jnp.float32, low / len(pieces), high / len(pieces)))
        level = level * jnp.repeat(steps, extent[dim] // parts).reshape([-1 if axis == dim else 1 for axis in range(len(extent))])
    return level


def deal_out(stream_key, own, number, rows, count, top, reach, lean):
    sequence = jax.random.permutation(stream_key, count)
    crowded, usual = load_shares(count, rows * top, reach, lean, True), load_shares(count, rows * top, reach, lean, False)
    places = jnp.arange(count)

    def named(sizes, turn):
        used = int((sizes > 0).sum())
        fixed = max(1, used // 4)
        passed = fixed + (places - fixed + turn * (used - fixed)) % max(1, count - fixed)
        return jnp.zeros((count,), jnp.int32).at[sequence[jnp.where(places < fixed, places, passed)]].set(jnp.asarray(sizes, jnp.int32))

    sizes = jnp.where(number % 4 == 0, named(crowded, number // 4), named(usual, number - number // 4 - 1))
    mixed = jax.random.permutation(jax.random.fold_in(own, 3), count)
    donor, sink = mixed[0:count // 2 * 2:2], mixed[1:count // 2 * 2:2]
    margin = jnp.minimum(sizes[donor] - 1, reach - sizes[sink]) // 2
    margin = jnp.where((donor == sequence[0]) | (sink == sequence[0]) | (sizes[sink] == 0), 0, jnp.maximum(margin, 0))
    passed = jax.random.randint(jax.random.fold_in(own, 4), (count // 2,), 0, 1 << 20) % (margin + 1)
    sizes = sizes.at[donor].add(-passed).at[sink].add(passed)
    labels = jnp.searchsorted(jnp.cumsum(sizes), jnp.arange(rows * top), side="right").astype(jnp.int32)
    listing = labels.reshape(top, rows).T
    listing = listing[jax.random.permutation(jax.random.fold_in(own, 1), rows)]
    turn = jax.random.randint(jax.random.fold_in(own, 2), (rows, 1), 0, top)
    return jnp.take_along_axis(listing, (jnp.arange(top)[None, :] + turn) % top, axis=1)


def load_shares(count, total, reach, lean, full):
    portions = [(1 << 20) // math.isqrt(rank ** lean) + 1 for rank in range(1, count + 1)]
    largest = reach if full else min(reach, max(-(-total // count), total * portions[0] // sum(portions)))
    least = 1 if total - largest >= count - 1 else 0
    holding, spare = [largest] + [least] * (count - 1), total - largest - least * (count - 1)
    while spare > 0:
        movable = [i for i in range(1, count) if holding[i] < largest] or [i for i in range(1, count) if holding[i] < reach]
        whole, left = sum([portions[i] for i in movable]), spare
        for i in movable:
            extra = min(reach - holding[i], max(1, left * portions[i] // whole), spare)
            holding[i] = holding[i] + extra
            spare = spare - extra
    return np.array(holding)


def scatter_about(own_key, dims, width, reach, split=(), kind=jnp.bfloat16):
    values = width * jax.random.normal(own_key, dims, jnp.float32)
    if split:
        values = values * levels(own_key, dims, split, -0.22, 0.18)
    return jnp.clip(values, -reach, reach).astype(kind)


def setup_inputs(seed: int = 0) -> dict:
    key_of = jax.random.split(jax.random.key(seed), 15)
    policy_hidden = scatter_about(key_of[0], (TOKENS, D), 1.0, 6.0, ((0, 16), (1, 8)))
    reference_hidden = scatter_about(key_of[1], (TOKENS, D), 1.0, 6.0, ((0, 16), (1, 8)))
    policy_norm_gain = jnp.clip(1.0 + 0.15 * jax.random.normal(key_of[2], (D,), jnp.float32), 0.25, 1.75)
    reference_norm_gain = jnp.clip(1.0 + 0.15 * jax.random.normal(key_of[3], (D,), jnp.float32), 0.25, 1.75)
    policy_router = draw_policy_router(jax.random.fold_in(key_of[14], 71), 0)
    reference_router = draw_reference_router(jax.random.fold_in(key_of[14], 71), 0)
    policy_gate = scatter_about(key_of[6], (EXPERTS, D, FF), D ** -0.5, 0.09375, ((0, 8), (1, 16)))
    policy_up = scatter_about(key_of[7], (EXPERTS, D, FF), D ** -0.5, 0.09375, ((0, 8), (1, 16)))
    policy_down = scatter_about(key_of[8], (EXPERTS, FF, D), FF ** -0.5, 0.0625, ((0, 8), (1, 16)))
    reference_gate = scatter_about(key_of[9], (EXPERTS, D, FF), D ** -0.5, 0.09375, ((0, 8), (1, 16)))
    reference_up = scatter_about(key_of[10], (EXPERTS, D, FF), D ** -0.5, 0.09375, ((0, 8), (1, 16)))
    reference_down = scatter_about(key_of[11], (EXPERTS, FF, D), FF ** -0.5, 0.0625, ((0, 8), (1, 16)))
    expert_ids_keys = jax.random.split(jax.random.fold_in(key_of[12], 1), TOKENS // TOK_DEV)
    expert_ids_turns = jax.random.permutation(jax.random.fold_in(key_of[12], 3), TOKENS // TOK_DEV)
    expert_ids = jax.vmap(lambda own, number: deal_out(jax.random.fold_in(key_of[12], 2), own, number, TOK_DEV, EXPERTS, TOP, CAP, 2))(expert_ids_keys, expert_ids_turns).reshape((TOKENS, TOP))
    lengths = draw_lengths(jax.random.fold_in(key_of[14], 71), 0)
    return {"policy_hidden": policy_hidden, "reference_hidden": reference_hidden, "policy_norm_gain": policy_norm_gain, "reference_norm_gain": reference_norm_gain, "policy_router": policy_router, "reference_router": reference_router, "policy_gate": policy_gate, "policy_up": policy_up, "policy_down": policy_down, "reference_gate": reference_gate, "reference_up": reference_up, "reference_down": reference_down, "expert_ids": expert_ids, "lengths": lengths}


EPSILON = 1e-05
KL_WEIGHT = 1.0
BALANCE_WEIGHT = 0.5

def normalize(hidden, norm_gain):
    values = hidden.astype(jnp.float32)
    meansq = lax.optimization_barrier(jnp.mean(values * values, axis=1, keepdims=True))
    return values * norm_gain * lax.rsqrt(meansq + EPSILON)

def expert_apply(operands):
    expert_rows, gate_weight, up_weight, down_weight = operands
    row_count = expert_rows.shape[0]
    gate_value = jnp.dot(expert_rows, gate_weight, preferred_element_type=jnp.float32)
    up_value = jnp.dot(expert_rows, up_weight, preferred_element_type=jnp.float32)
    hidden = (jax.nn.silu(gate_value) * up_value).astype(jnp.bfloat16)
    block_width = FF // N_DP
    hidden_blocks = hidden.reshape(row_count, N_DP, block_width).transpose(1, 0, 2)
    down_blocks = down_weight.reshape(N_DP, block_width, D)

    def add_block(running_total, operand_pair):
        block_part = jnp.dot(operand_pair[0], operand_pair[1], preferred_element_type=jnp.float32).astype(jnp.bfloat16)
        block_part = lax.optimization_barrier(block_part)
        return (running_total + block_part.astype(jnp.float32), None)
    running_total, _ = lax.scan(add_block, jnp.zeros((row_count, D), jnp.float32), (hidden_blocks, down_blocks))
    return running_total.astype(jnp.bfloat16)

def model_mixture(hidden, norm_gain, router, gate_weight, up_weight, down_weight, flat_slot, expert_ids, live_mask):
    normed = normalize(hidden, norm_gain)
    logits = jnp.dot(normed, router, precision=lax.Precision.HIGHEST)
    token_rows = normed.astype(jnp.bfloat16)
    route_rows = jnp.repeat(token_rows, TOP, axis=0)
    buffer = jnp.zeros((EXPERTS * N_DP * CAP, D), jnp.bfloat16).at[flat_slot].set(route_rows)
    buffer = buffer.reshape(EXPERTS, N_DP * CAP, D)
    outputs = lax.map(expert_apply, (buffer, gate_weight, up_weight, down_weight))
    picked = outputs.reshape(EXPERTS * N_DP * CAP, D)[flat_slot].reshape(TOKENS, TOP, D)
    matches = expert_ids[:, :, None] == jnp.arange(EXPERTS, dtype=jnp.int32)[None, None, :]
    chosen = lax.optimization_barrier(jnp.sum(jnp.where(matches, logits[:, None, :], 0.0), axis=2))
    gates = jax.nn.softmax(chosen, axis=1)
    mixed_rows = lax.optimization_barrier(jnp.sum(picked.astype(jnp.float32) * gates[:, :, None], axis=1)) * live_mask[:, None]
    return (mixed_rows.astype(jnp.bfloat16), logits)

def reference(policy_hidden, reference_hidden, policy_norm_gain, reference_norm_gain, policy_router, reference_router, policy_gate, policy_up, policy_down, reference_gate, reference_up, reference_down, expert_ids, lengths):
    position = jnp.arange(TOKENS, dtype=jnp.int32)
    live_mask = (position % SEG < jnp.repeat(lengths, SEG)).astype(jnp.float32)
    block_ids = expert_ids.reshape(N_DP, TOK_DEV * TOP)
    onehot = (block_ids[:, :, None] == jnp.arange(EXPERTS, dtype=jnp.int32)[None, None, :]).astype(jnp.int32)
    before = jnp.cumsum(onehot, axis=1) - onehot
    within = lax.optimization_barrier(jnp.sum(before * onehot, axis=2))
    block_index = jnp.arange(N_DP, dtype=jnp.int32)[:, None]
    flat_slot = (block_ids * (N_DP * CAP) + block_index * CAP + within).reshape(-1).astype(jnp.int32)
    policy_mixture, policy_logits = model_mixture(policy_hidden, policy_norm_gain, policy_router, policy_gate, policy_up, policy_down, flat_slot, expert_ids, live_mask)
    reference_mixture, reference_logits = model_mixture(reference_hidden, reference_norm_gain, reference_router, reference_gate, reference_up, reference_down, flat_slot, expert_ids, live_mask)
    policy_logprob = jax.nn.log_softmax(policy_logits, axis=1)
    reference_logprob = jax.nn.log_softmax(reference_logits, axis=1)
    policy_prob = jnp.exp(policy_logprob)
    token_kl = lax.optimization_barrier(jnp.sum(policy_prob * (policy_logprob - reference_logprob), axis=1)) * live_mask
    route_onehot = onehot.reshape(TOKENS, TOP, EXPERTS)
    counts = lax.optimization_barrier(jnp.sum(lax.optimization_barrier(jnp.sum(route_onehot, axis=1)).astype(jnp.float32) * live_mask[:, None], axis=0))
    probsum = lax.optimization_barrier(jnp.sum(policy_prob * live_mask[:, None], axis=0))
    kl_total = jnp.sum(token_kl)
    token_total = float(TOKENS)
    balance = EXPERTS * jnp.sum(counts / (TOP * token_total) * probsum / token_total)
    loss = KL_WEIGHT * kl_total / token_total + BALANCE_WEIGHT * balance
    return (policy_mixture, reference_mixture, token_kl, loss)
```

```python
import jax
import jax.numpy as jnp
from jax import lax
from jax.experimental import pallas as pl
from jax.sharding import Mesh
from jax.sharding import PartitionSpec as P

D = 4096
SEG = 32
ROW = "dp_y"
COLUMN = "dp_z"
CORE = "dp_core"
DP = (ROW, COLUMN, CORE)


EPSILON = 1e-05
KL_WEIGHT = 1.0
BALANCE_WEIGHT = 0.5
PACK = 4


def pack_kernel(gate_ref, up_ref, *packed_refs):
    parts = len(packed_refs)
    width = gate_ref.shape[1] // (PACK * parts)
    for k in range(PACK):
        for part, packed_ref in enumerate(packed_refs):
            taken = slice((k * parts + part) * width, (k * parts + part + 1) * width)
            packed_ref[k, :, :width] = gate_ref[:, taken]
            packed_ref[k, :, width:] = up_ref[:, taken]


def packed(gate, up, peers, parts):
    rows, width = gate.shape[1:]
    piece = width // peers
    taken = pl.BlockSpec((None, rows, PACK * piece), lambda j: (0, 0, j))
    return pl.pallas_call(
        pack_kernel,
        grid=(peers // PACK,),
        in_specs=[taken, taken],
        out_specs=[pl.BlockSpec((PACK, rows, 2 * piece // parts), lambda j: (j, 0, 0))] * parts,
        out_shape=[jax.ShapeDtypeStruct((peers, rows, 2 * piece // parts), gate.dtype)] * parts,
        cost_estimate=pl.CostEstimate(
            flops=0, bytes_accessed=8 * rows * width, transcendentals=0
        ),
    )(gate, up)


def router_terms(hidden, norm_gain, router):
    values = hidden.astype(jnp.float32)
    partial_logits = jnp.dot(values * norm_gain, router, precision=lax.Precision.HIGHEST)
    return (partial_logits, jnp.sum(values * values, axis=1))


def exchange(value, axis):
    return lax.all_to_all(value, axis, split_axis=0, concat_axis=0, tiled=True)


def from_xor(value, axis, step):
    return lax.ppermute(value, axis, [(i, i ^ step) for i in range(lax.axis_size(axis))])


def from_ahead(value, axis, step):
    size = lax.axis_size(axis)
    return lax.ppermute(value, axis, [((i + step) % size, i) for i in range(size)])


def of_everyone(value, *axes):
    for axis in axes:
        step = 1
        while step < lax.axis_size(axis):
            value = value + from_xor(value, axis, step)
            step *= 2
    return value


def chip_pair(own):
    return jnp.stack((own, from_xor(own, COLUMN, 1)))


def all_chips(pair):
    ahead, behind = from_ahead(pair, ROW, 1), from_ahead(pair, ROW, 3)
    return (pair, ahead, from_ahead(pair, ROW, 2), behind)


def gathered(chips):
    pieces = (*chips, *(from_xor(chip, CORE, 1) for chip in chips))
    models, slot_count, width = chips[0].shape[1:]
    return [
        jnp.concatenate([piece[:, m].reshape(-1, width) for piece in pieces])
        for m in range(models)
    ]


def split_in_three(values):
    rows = []
    for _ in range(3):
        rows.append(values.astype(jnp.bfloat16))
        values = values - rows[-1].astype(jnp.float32)
    return jnp.stack(rows)


def normed_rows(arrived, gain):
    values = arrived.astype(jnp.float32)
    scale = lax.rsqrt(jnp.sum(values * values, axis=(0, 2)) / D + EPSILON)
    normed = (values * gain[:, None, :] * scale[None, :, None]).astype(jnp.bfloat16)
    return normed.transpose(1, 0, 2).reshape(arrived.shape[1], -1)


def hidden_units(rows, gate_up):
    both = jnp.dot(rows, gate_up, preferred_element_type=jnp.float32)
    width = both.shape[1] // 2
    return (jax.nn.silu(both[:, :width]) * both[:, width:]).astype(jnp.bfloat16)


def added(*terms):
    total = terms[0].astype(jnp.float32)
    for term in terms[1:]:
        total = total + term.astype(jnp.float32)
    return total.astype(jnp.bfloat16)


def chip_terms(hidden, down):
    half = hidden.shape[0] // 2

    def part(rows):
        return jnp.dot(rows, down, preferred_element_type=jnp.float32)

    arrived = from_xor(part(hidden[half:]).astype(jnp.bfloat16), CORE, 1)
    return added(part(hidden[:half]), arrived).reshape(lax.axis_size(ROW), -1, down.shape[1])


def toward_neighbours(chip):
    middle = chip.shape[2] // 2
    left, right = chip[2, :, :middle], chip[2, :, middle:]
    ahead = jnp.concatenate(
        (added(chip[1, :, :middle], from_ahead(left, ROW, 3)), chip[1, :, middle:]), axis=1
    )
    behind = jnp.concatenate(
        (chip[3, :, :middle], added(chip[3, :, middle:], from_ahead(right, ROW, 1))), axis=1
    )
    return (ahead, behind)


def row_terms(own, ahead, behind):
    return added(own, from_ahead(ahead, ROW, 3), from_ahead(behind, ROW, 1))


def column_terms(row):
    half = row.shape[0] // 2
    return added(row[:half], from_xor(row[half:], COLUMN, 1))


def per_device(
    policy_hidden,
    reference_hidden,
    policy_norm_gain,
    reference_norm_gain,
    policy_router,
    reference_router,
    policy_gate,
    policy_up,
    policy_down,
    reference_gate,
    reference_up,
    reference_down,
    expert_ids,
    lengths,
):
    expert_count = lax.axis_size("expert")
    peers = lax.axis_size(DP)
    token_count, feature_block = policy_hidden.shape
    route_count = expert_ids.shape[1]
    slot_count = 3 * token_count // expert_count
    token_total = float(token_count * peers)

    policy_partial, policy_squares = router_terms(policy_hidden, policy_norm_gain, policy_router)
    reference_partial, reference_squares = router_terms(
        reference_hidden, reference_norm_gain, reference_router
    )
    sums = of_everyone(
        jnp.concatenate(
            (policy_partial.T, reference_partial.T, policy_squares[None], reference_squares[None])
        ),
        "expert",
    ).T
    policy_scale = lax.rsqrt(sums[:, 2 * expert_count] / D + EPSILON)[:, None]
    reference_scale = lax.rsqrt(sums[:, 2 * expert_count + 1] / D + EPSILON)[:, None]
    policy_logits = sums[:, :expert_count] * policy_scale
    reference_logits = sums[:, expert_count : 2 * expert_count] * reference_scale
    flat_ids = expert_ids.reshape(-1)
    onehot = (flat_ids[:, None] == jnp.arange(expert_count, dtype=jnp.int32)[None, :]).astype(
        jnp.int32
    )
    before = jnp.cumsum(onehot, axis=0) - onehot
    within = jnp.sum(before * onehot, axis=1)
    slot_index = jnp.arange(expert_count * slot_count, dtype=jnp.int32)
    target = (flat_ids * slot_count + within).reshape(token_count, route_count)
    select = jnp.any(slot_index[:, None, None] == target[None, :, :], axis=2)
    placed = jnp.dot(
        select.astype(jnp.bfloat16),
        jnp.concatenate((policy_hidden, reference_hidden), axis=1),
        preferred_element_type=jnp.float32,
    ).astype(jnp.bfloat16)
    gain_rows = split_in_three(jnp.concatenate((policy_norm_gain, reference_norm_gain)))
    gain_rows = jnp.pad(gain_rows, ((0, 13), (0, 0)))
    arrived = exchange(
        jnp.concatenate(
            (
                placed.reshape(expert_count, slot_count, 2 * feature_block),
                jnp.broadcast_to(gain_rows, (expert_count, *gain_rows.shape)),
            ),
            axis=1,
        ),
        "expert",
    )
    gains = jnp.sum(arrived[:, slot_count : slot_count + 3].astype(jnp.float32), axis=1)
    arrived = arrived[:, :slot_count]
    live_mask = (
        (jnp.arange(SEG, dtype=jnp.int32)[None, :] < lengths[:, None])
        .reshape(-1)
        .astype(jnp.float32)
    )
    chosen_slot = target[:, :, None] == slot_index[None, None, :]

    def slot_weights(logits):
        matches = expert_ids[:, :, None] == jnp.arange(expert_count, dtype=jnp.int32)[None, None, :]
        chosen = jnp.sum(jnp.where(matches, logits[:, None, :], 0.0), axis=2)
        gates = jax.nn.softmax(chosen, axis=1) * live_mask[:, None]
        return jnp.sum(jnp.where(chosen_slot, gates[:, :, None], 0.0), axis=1)

    policy_weights = slot_weights(policy_logits)
    reference_weights = slot_weights(reference_logits)
    policy_logprob = jax.nn.log_softmax(policy_logits, axis=1)
    reference_logprob = jax.nn.log_softmax(reference_logits, axis=1)
    policy_prob = jnp.exp(policy_logprob)
    token_kl = jnp.sum(policy_prob * (policy_logprob - reference_logprob), axis=1) * live_mask
    route_onehot = onehot.reshape(token_count, route_count, expert_count)
    counts = jnp.sum(jnp.sum(route_onehot, axis=1).astype(jnp.float32) * live_mask[:, None], axis=0)
    probsum = jnp.sum(policy_prob * live_mask[:, None], axis=0)
    local_totals = jnp.concatenate((counts, probsum, jnp.sum(token_kl)[None]))

    own = jnp.stack(
        (
            normed_rows(arrived[:, :, :feature_block], gains[:, :feature_block]),
            normed_rows(arrived[:, :, feature_block:], gains[:, feature_block:]),
        )
    )
    (policy_packed,) = packed(policy_gate, policy_up, peers, 1)
    first_packed, second_packed = packed(reference_gate, reference_up, peers, 2)
    policy_gate_up = exchange(policy_packed, DP).reshape(D, -1)
    totals = local_totals + from_xor(local_totals, ROW, 1)
    pair, totals, policy_weights, reference_weights, policy_gate_up, first_packed, second_packed = (
        lax.optimization_barrier(
            (
                chip_pair(own),
                totals,
                policy_weights,
                reference_weights,
                policy_gate_up,
                first_packed,
                second_packed,
            )
        )
    )

    first_gate_up = exchange(first_packed, DP).reshape(D, -1)
    policy_rows, reference_rows = gathered(all_chips(pair))
    policy_chip = chip_terms(hidden_units(policy_rows, policy_gate_up), policy_down[0])
    totals = totals + from_xor(totals, ROW, 2)
    policy_chip, totals, first_gate_up, second_packed = lax.optimization_barrier(
        (policy_chip, totals, first_gate_up, second_packed)
    )

    second_gate_up = exchange(second_packed, DP).reshape(D, -1)
    first_hidden = hidden_units(reference_rows, first_gate_up)
    policy_row = row_terms(policy_chip[0], *toward_neighbours(policy_chip))
    totals = totals + from_xor(totals, COLUMN, 1)
    first_hidden, policy_row, totals, second_gate_up = lax.optimization_barrier(
        (first_hidden, policy_row, totals, second_gate_up)
    )

    second_hidden = hidden_units(reference_rows, second_gate_up)
    reference_chip = chip_terms(
        jnp.concatenate((first_hidden, second_hidden), axis=1), reference_down[0]
    )
    policy_output = column_terms(policy_row)
    reference_row = row_terms(reference_chip[0], *toward_neighbours(reference_chip))
    reference_output = column_terms(reference_row)
    totals = totals + from_xor(totals, CORE, 1)
    counts, probsum = totals[:expert_count], totals[expert_count : 2 * expert_count]
    kl_total = totals[2 * expert_count]
    balance = expert_count * jnp.sum(counts / (route_count * token_total) * probsum / token_total)
    loss = KL_WEIGHT * kl_total / token_total + BALANCE_WEIGHT * balance
    outputs = jnp.stack((policy_output, reference_output), axis=1)
    outputs = outputs.reshape(slot_count, 2, expert_count, feature_block).transpose(2, 0, 1, 3)
    outputs = exchange(outputs.reshape(expert_count, slot_count, -1), "expert")
    outputs = outputs.reshape(expert_count * slot_count, -1)

    def mixture(weights, output):
        mixed = jnp.dot(weights, output.astype(jnp.float32), precision=lax.Precision.HIGHEST)
        return mixed.astype(jnp.bfloat16)

    policy_mixture = mixture(policy_weights, outputs[:, :feature_block])
    reference_mixture = mixture(reference_weights, outputs[:, feature_block:])
    return (policy_mixture, reference_mixture, token_kl, loss)


def solution(mesh):
    split = Mesh(mesh.devices.reshape(4, 2, 2, mesh.shape["expert"]), (*DP, "expert"))
    placed = (
        P(DP, "expert"),
        P(DP, "expert"),
        P("expert"),
        P("expert"),
        P("expert", None),
        P("expert", None),
        P("expert", DP, None),
        P("expert", DP, None),
        P("expert", DP, None),
        P("expert", DP, None),
        P("expert", DP, None),
        P("expert", DP, None),
        P(DP, None),
        P(DP),
    )
    return jax.shard_map(
        per_device,
        mesh=split,
        in_specs=placed,
        out_specs=(P(DP, "expert"), P(DP, "expert"), P(DP), P()),
        check_vma=False,
    )
```

```python
import jax
import jax.numpy as jnp
from jax import lax
from jax.experimental import pallas as pl
from jax.sharding import Mesh
from jax.sharding import PartitionSpec as P

D = 4096
SEG = 32
ROW = "dp_y"
COLUMN = "dp_z"
CORE = "dp_core"
DP = (ROW, COLUMN, CORE)


EPSILON = 1e-05
KL_WEIGHT = 1.0
BALANCE_WEIGHT = 0.5
PACK = 2


def pack_kernel(*refs):
    packed_ref = refs[-1]
    piece = refs[0].shape[1] // PACK
    for k in range(PACK):
        for place, ref in enumerate(refs[:-1]):
            packed_ref[k, :, place * piece : (place + 1) * piece] = ref[
                :, k * piece : (k + 1) * piece
            ]


def packed(weights, peers):
    rows, width = weights[0].shape[1:]
    piece = width // peers
    taken = pl.BlockSpec((None, rows, PACK * piece), lambda j: (0, 0, j))
    wide = len(weights) * piece
    return pl.pallas_call(
        pack_kernel,
        grid=(peers // PACK,),
        in_specs=[taken] * len(weights),
        out_specs=pl.BlockSpec((PACK, rows, wide), lambda j: (j, 0, 0)),
        out_shape=jax.ShapeDtypeStruct((peers, rows, wide), weights[0].dtype),
        cost_estimate=pl.CostEstimate(
            flops=0, bytes_accessed=4 * len(weights) * rows * width, transcendentals=0
        ),
    )(*weights)


def router_terms(hidden, norm_gain, router):
    values = hidden.astype(jnp.float32)
    partial_logits = jnp.dot(values * norm_gain, router, precision=lax.Precision.HIGHEST)
    return (partial_logits, jnp.sum(values * values, axis=1))


def exchange(value, axis):
    return lax.all_to_all(value, axis, split_axis=0, concat_axis=0, tiled=True)


def from_xor(value, axis, step):
    return lax.ppermute(value, axis, [(i, i ^ step) for i in range(lax.axis_size(axis))])


def from_ahead(value, axis, step):
    size = lax.axis_size(axis)
    return lax.ppermute(value, axis, [((i + step) % size, i) for i in range(size)])


def of_everyone(value, *axes):
    for axis in axes:
        step = 1
        while step < lax.axis_size(axis):
            value = value + from_xor(value, axis, step)
            step *= 2
    return value


def row_blocks(own):
    ahead, behind, far = (from_ahead(own, ROW, k) for k in (1, 3, 2))
    return (own, ahead, far, behind)


def gathered(policy_own, reference_own):
    pair = jnp.stack((policy_own, from_xor(policy_own, COLUMN, 1)))
    row = jnp.stack(row_blocks(reference_own))
    columns = (row, from_xor(row, COLUMN, 1))
    return (both_cores(row_blocks(pair)), columns)


def both_cores(pieces):
    pieces = (*pieces, *(from_xor(piece, CORE, 1) for piece in pieces))
    return jnp.concatenate([piece.reshape(-1, piece.shape[-1]) for piece in pieces])


def split_in_three(values):
    rows = []
    for _ in range(3):
        rounded = lax.reduce_precision(values, exponent_bits=8, mantissa_bits=7)
        rows.append(rounded.astype(jnp.bfloat16))
        values = values - rounded
    return jnp.stack(rows)


def normed_rows(arrived, gain):
    values = arrived.astype(jnp.float32)
    scale = lax.rsqrt(jnp.sum(values * values, axis=(0, 2)) / D + EPSILON)
    normed = (values * gain[:, None, :] * scale[None, :, None]).astype(jnp.bfloat16)
    return normed.transpose(1, 0, 2).reshape(arrived.shape[1], -1)


def hidden_units(rows, gate_up):
    both = jnp.dot(rows, gate_up, preferred_element_type=jnp.float32)
    width = both.shape[1] // 2
    return (jax.nn.silu(both[:, :width]) * both[:, width:]).astype(jnp.bfloat16)


def added(*terms):
    total = terms[0].astype(jnp.float32)
    for term in terms[1:]:
        total = total + term.astype(jnp.float32)
    return total.astype(jnp.bfloat16)


def core_terms(hidden, down):
    return jnp.dot(hidden, down, preferred_element_type=jnp.float32)


def chip_terms(mine, sent):
    return added(mine, from_xor(sent, CORE, 1)).reshape(lax.axis_size(ROW), -1, mine.shape[1])


def from_two_away(chip):
    middle = chip.shape[2] // 2
    return (from_ahead(chip[2, :, :middle], ROW, 3), from_ahead(chip[2, :, middle:], ROW, 1))


def toward_neighbours(chip, left, right):
    middle = chip.shape[2] // 2
    ahead = jnp.concatenate((added(chip[1, :, :middle], left), chip[1, :, middle:]), axis=1)
    behind = jnp.concatenate((chip[3, :, :middle], added(chip[3, :, middle:], right)), axis=1)
    return (ahead, behind)


def row_terms(own, ahead, behind):
    return added(own, from_ahead(ahead, ROW, 3), from_ahead(behind, ROW, 1))


def column_terms(row):
    half = row.shape[0] // 2
    return added(row[:half], from_xor(row[half:], COLUMN, 1))


def per_device(
    policy_hidden,
    reference_hidden,
    policy_norm_gain,
    reference_norm_gain,
    policy_router,
    reference_router,
    policy_gate,
    policy_up,
    policy_down,
    reference_gate,
    reference_up,
    reference_down,
    expert_ids,
    lengths,
):
    expert_count = lax.axis_size("expert")
    peers = lax.axis_size(DP)
    token_count, feature_block = policy_hidden.shape
    route_count = expert_ids.shape[1]
    slot_count = 3 * token_count // expert_count
    token_total = float(token_count * peers)

    policy_partial, policy_squares = router_terms(policy_hidden, policy_norm_gain, policy_router)
    reference_partial, reference_squares = router_terms(
        reference_hidden, reference_norm_gain, reference_router
    )
    sums = jnp.concatenate(
        (policy_partial.T, reference_partial.T, policy_squares[None], reference_squares[None])
    )

    flat_ids = expert_ids.reshape(-1)
    onehot = (flat_ids[:, None] == jnp.arange(expert_count, dtype=jnp.int32)[None, :]).astype(
        jnp.int32
    )
    before = jnp.cumsum(onehot, axis=0) - onehot
    within = jnp.sum(before * onehot, axis=1)
    slot_index = jnp.arange(expert_count * slot_count, dtype=jnp.int32)
    target = (flat_ids * slot_count + within).reshape(token_count, route_count)
    select = jnp.any(slot_index[:, None, None] == target[None, :, :], axis=2)
    placed = jnp.dot(
        select.astype(jnp.bfloat16),
        jnp.concatenate((policy_hidden, reference_hidden), axis=1),
        preferred_element_type=jnp.float32,
    ).astype(jnp.bfloat16)
    small = jnp.concatenate((policy_norm_gain, reference_norm_gain, sums.ravel()))
    small_rows = -(-small.size // (2 * feature_block))
    small = jnp.pad(small, (0, small_rows * 2 * feature_block - small.size))
    small = split_in_three(small.reshape(small_rows, -1)).reshape(3 * small_rows, -1)
    small = jnp.pad(small, ((0, -3 * small_rows % 16), (0, 0)))
    arrived = exchange(
        jnp.concatenate(
            (
                placed.reshape(expert_count, slot_count, 2 * feature_block),
                jnp.broadcast_to(small, (expert_count, *small.shape)),
            ),
            axis=1,
        ),
        "expert",
    )
    weights = packed((policy_gate, policy_up, reference_gate, reference_up), peers)
    arrived, weights = lax.optimization_barrier((arrived, weights))
    small = arrived[:, slot_count : slot_count + 3 * small_rows].astype(jnp.float32)
    small = jnp.sum(small.reshape(expert_count, 3, -1), axis=1)
    gains = small[:, : 2 * feature_block]
    sums = jnp.sum(small[:, 2 * feature_block : 2 * feature_block + sums.size], axis=0)
    arrived = arrived[:, :slot_count]
    policy_rows, reference_columns = gathered(
        normed_rows(arrived[:, :, :feature_block], gains[:, :feature_block]),
        normed_rows(arrived[:, :, feature_block:], gains[:, feature_block:]),
    )
    sums = sums.reshape(2 * expert_count + 2, token_count).T
    policy_scale = lax.rsqrt(sums[:, 2 * expert_count] / D + EPSILON)[:, None]
    reference_scale = lax.rsqrt(sums[:, 2 * expert_count + 1] / D + EPSILON)[:, None]
    policy_logits = sums[:, :expert_count] * policy_scale
    reference_logits = sums[:, expert_count : 2 * expert_count] * reference_scale
    live_mask = (
        (jnp.arange(SEG, dtype=jnp.int32)[None, :] < lengths[:, None])
        .reshape(-1)
        .astype(jnp.float32)
    )
    chosen_slot = target[:, :, None] == slot_index[None, None, :]

    def slot_weights(logits):
        matches = expert_ids[:, :, None] == jnp.arange(expert_count, dtype=jnp.int32)[None, None, :]
        chosen = jnp.sum(jnp.where(matches, logits[:, None, :], 0.0), axis=2)
        gates = jax.nn.softmax(chosen, axis=1) * live_mask[:, None]
        return jnp.sum(jnp.where(chosen_slot, gates[:, :, None], 0.0), axis=1)

    policy_weights = slot_weights(policy_logits)
    reference_weights = slot_weights(reference_logits)
    policy_logprob = jax.nn.log_softmax(policy_logits, axis=1)
    reference_logprob = jax.nn.log_softmax(reference_logits, axis=1)
    policy_prob = jnp.exp(policy_logprob)
    token_kl = jnp.sum(policy_prob * (policy_logprob - reference_logprob), axis=1) * live_mask
    route_onehot = onehot.reshape(token_count, route_count, expert_count)
    counts = jnp.sum(jnp.sum(route_onehot, axis=1).astype(jnp.float32) * live_mask[:, None], axis=0)
    probsum = jnp.sum(policy_prob * live_mask[:, None], axis=0)
    local_totals = jnp.concatenate((counts, probsum, jnp.sum(token_kl)[None]))

    (
        policy_rows,
        reference_columns,
        policy_weights,
        reference_weights,
        token_kl,
        local_totals,
        weights,
    ) = lax.optimization_barrier(
        (
            policy_rows,
            reference_columns,
            policy_weights,
            reference_weights,
            token_kl,
            local_totals,
            weights,
        )
    )
    gate_up = exchange(weights, DP).reshape(D, -1)
    (
        gate_up,
        policy_rows,
        reference_columns,
        policy_weights,
        reference_weights,
        token_kl,
        local_totals,
    ) = lax.optimization_barrier(
        (
            gate_up,
            policy_rows,
            reference_columns,
            policy_weights,
            reference_weights,
            token_kl,
            local_totals,
        )
    )
    width = policy_down.shape[1]
    half = policy_rows.shape[0] // 2
    policy_units = hidden_units(policy_rows, gate_up[:, : 2 * width])
    policy_sent = core_terms(policy_units[half:], policy_down[0]).astype(jnp.bfloat16)
    policy_chip = chip_terms(core_terms(policy_units[:half], policy_down[0]), policy_sent)
    policy_chip, reference_columns = lax.optimization_barrier((policy_chip, reference_columns))
    reference_units = hidden_units(both_cores(reference_columns), gate_up[:, 2 * width :])
    reference_units = reference_units.reshape(
        lax.axis_size(CORE), lax.axis_size(COLUMN), lax.axis_size(ROW), slot_count, width
    )
    reference_units = reference_units.swapaxes(1, 2).reshape(-1, width)
    totals = local_totals + from_xor(local_totals, ROW, 1)
    passing, reference_units, totals = lax.optimization_barrier(
        (from_two_away(policy_chip), reference_units, totals)
    )
    policy_row = row_terms(policy_chip[0], *toward_neighbours(policy_chip, *passing))
    reference_sent = core_terms(reference_units[half:], reference_down[0]).astype(jnp.bfloat16)
    reference_chip = chip_terms(
        core_terms(reference_units[:half], reference_down[0]), reference_sent
    )

    totals = totals + from_xor(totals, ROW, 2)
    reference_chip, totals = lax.optimization_barrier((reference_chip, totals))
    totals = of_everyone(totals, COLUMN, CORE)
    counts, probsum = totals[:expert_count], totals[expert_count : 2 * expert_count]
    kl_total = totals[2 * expert_count]
    balance = expert_count * jnp.sum(counts / (route_count * token_total) * probsum / token_total)
    loss = KL_WEIGHT * kl_total / token_total + BALANCE_WEIGHT * balance
    def mixture(weights, output):
        output = output.reshape(slot_count, expert_count, feature_block).swapaxes(0, 1)
        output = exchange(output, "expert").reshape(expert_count * slot_count, -1)
        mixed = jnp.dot(weights, output.astype(jnp.float32), precision=lax.Precision.HIGHEST)
        return mixed.astype(jnp.bfloat16)

    policy_mixture = mixture(policy_weights, column_terms(policy_row))
    reference_row = row_terms(reference_chip[0], *toward_neighbours(reference_chip, *from_two_away(reference_chip)))
    reference_row, policy_mixture, reference_weights, loss = lax.optimization_barrier(
        (reference_row, policy_mixture, reference_weights, loss)
    )
    reference_mixture = mixture(reference_weights, column_terms(reference_row))
    return (policy_mixture, reference_mixture, token_kl, loss)


def solution(mesh):
    split = Mesh(mesh.devices.reshape(4, 2, 2, mesh.shape["expert"]), (*DP, "expert"))
    placed = (
        P(DP, "expert"),
        P(DP, "expert"),
        P("expert"),
        P("expert"),
        P("expert", None),
        P("expert", None),
        P("expert", DP, None),
        P("expert", DP, None),
        P("expert", DP, None),
        P("expert", DP, None),
        P("expert", DP, None),
        P("expert", DP, None),
        P(DP, None),
        P(DP),
    )
    return jax.shard_map(
        per_device,
        mesh=split,
        in_specs=placed,
        out_specs=(P(DP, "expert"), P(DP, "expert"), P(DP), P()),
        check_vma=False,
    )
```
